32 devices in a mesh: grp: 2 (over core), aux: 4 (over y, x), orb: 4 (over z).
Axes of the slice: x: 2, y: 2, z: 4, core: 2. Of those that a mesh axis runs over, the one named last changes fastest.
Arguments:
- fitted_tensor: bfloat16 [4, 8192, 8192], P('grp', 'aux', 'orb'), may hold values from -0.23925781 to 0.23925781
- block_mask: int32 [2, 64, 64], P('grp'), may hold values 0 or 1
- orbitals: bfloat16 [8192, 256], P('aux'), may hold values from -0.0625 to 0.0625
- nuclear: float32 [8192], replicated, may hold values from 0.5 to 1.5
- centres: float32 [3, 8192], replicated, may hold values from 0 to 8
- mm_positions: float32 [3, 32768], P(None, ('grp', 'aux', 'orb')), may hold values from 0 to 8
- mm_charges: float32 [32768], P(('grp', 'aux', 'orb')), may hold values from -0.12 to 0.12
- neighbours: int32 [32, 2], P(('grp', 'aux', 'orb')), may hold values from 0 to 63, all different within a row
Outputs:
- fock: float32 [8192, 8192], P(('aux', 'orb'))
- mm_potential: float32 [32768], P(('grp', 'aux', 'orb'))
The draws below stay inside these ranges and needn't reach their ends.
Inputs may be any that keep to these rules, and one draw needn't show every extreme that they name: `neighbours`: each row names 2 different blocks; every block is named by some row.
All inputs are finite; a program needn't handle non-finite values. No bound on the sum of `block_mask` on one device may be relied on, other than what follows from the above.
Results may differ from the reference program's by a relative error of at most 0.01.
Values may be sent and summed in bfloat16 or wider, within the bound.
A program may use at most 128 MiB of HBM per device.

```python
import jax
import jax.numpy as jnp
from jax import lax

BLK = 128
NBF = 8192
NBLK = 64
PH = 2
SLABS = 2
NAUX = 4
NOCC = 256
MD = 1024
NMMBLK = 32
NMM = 32768
NB = 2


def plant(drawn, own_key, smallest, largest):
    spot = [jax.random.randint(jax.random.fold_in(own_key, axis), (), 0, length) for axis, length in enumerate(drawn.shape)]
    main_axis = drawn.shape.index(max(drawn.shape))
    next_to = spot[:main_axis] + [(spot[main_axis] + 1) % drawn.shape[main_axis]] + spot[main_axis + 1:]
    return drawn.at[tuple(spot)].set(smallest).at[tuple(next_to)].set(largest)


def level_of(stream_key, shape, split, low, largest):
    def one(position, parts):
        heights = jax.random.uniform(jax.random.fold_in(jax.random.fold_in(stream_key, 6), position), (parts,), jnp.float32, low / len(split), largest / len(split))
        return jnp.repeat(jnp.exp(heights), shape[position] // parts).reshape((-1,) + (1,) * (len(shape) - position - 1))

    factor_of = one(*split[0])
    for cut in split[1:]:
        factor_of = factor_of * one(*cut)
    return factor_of


def choose_distinct(key, rows, amount, top, lift):
    sequence = jax.random.permutation(jax.random.fold_in(key, 1), amount)
    pull = sequence
    for power in range(3):
        pull = pull * pull // amount
    pull = pull * lift // amount
    lots = jax.random.randint(jax.random.fold_in(key, 2), (rows, amount), 0, 4096) + pull
    sure = jax.random.permutation(jax.random.fold_in(key, 3), rows)[jnp.arange(amount) % rows]
    lots = jnp.where(jnp.arange(rows)[:, None] == sure[None, :], 1 << 14, lots)
    score = lots * amount + jnp.arange(amount)
    return lax.top_k(score.astype(jnp.int32), top)[1].astype(jnp.int32)


def normal_values(own_key, dims, width, limit, pieces=(), kind=jnp.bfloat16):
    gain = level_of(own_key, dims, pieces, -0.22, 0.18) if pieces else 1.0
    entries = jax.random.normal(own_key, dims, jnp.float32) * width * gain
    return jnp.minimum(jnp.maximum(entries, -limit), limit).astype(kind)


def setup_inputs(seed: int = 0) -> dict:
    key_list = jax.random.split(jax.random.key(seed), 9)
    return {
        "fitted_tensor": normal_values(key_list[0], (NAUX, NBF, NBF), 0.04, 0.23925781, ((0, 2), (1, 4), (2, 4))),
        "block_mask": plant((jax.random.randint(key_list[1], (SLABS, NBLK, NBLK), 0, 4) < 3).astype(jnp.int32), jax.random.fold_in(key_list[1], 1), 0, 1),
        "orbitals": normal_values(key_list[2], (NBF, NOCC), NBF ** -0.5, 0.0625, ((0, 4),)),
        "nuclear": jnp.clip(jax.random.uniform(key_list[3], (NBF,), jnp.float32, 0.5, 1.5), 0.5, 1.5),
        "centres": jnp.clip(jax.random.uniform(key_list[4], (3, NBF), jnp.float32, 0.0, 8.0), 0.0, 8.0),
        "mm_positions": jnp.clip(8.0 * jax.random.uniform(key_list[5], (3, NMM), jnp.float32) ** level_of(key_list[5], (3, NMM), ((1, 32),), -0.2, 0.2), 0.0, 8.0),
        "mm_charges": normal_values(key_list[6], (NMM,), 0.02, 0.12, ((0, 32),), jnp.float32),
        "neighbours": choose_distinct(key_list[7], NMMBLK, NBLK, NB, 256),
    }


softening = 1.0

def near_kernel(picker, centre_blocks, charge_blocks, atom_xyz):
    near_xyz = jnp.einsum('kb,cbj->ckj', picker, centre_blocks, precision=lax.Precision.HIGHEST)
    near_xyz = near_xyz.reshape(3, picker.shape[0] * centre_blocks.shape[2])
    near_q = jnp.dot(picker, charge_blocks, precision=lax.Precision.HIGHEST).reshape(-1)
    offsets = near_xyz[:, :, None] - atom_xyz[:, None, :]
    kernel = lax.rsqrt(lax.optimization_barrier(jnp.sum(offsets * offsets, axis=0)) + softening)
    return (kernel, near_q)

def reference(fitted_tensor, block_mask, orbitals, nuclear, centres, mm_positions, mm_charges, neighbours):
    c_full = orbitals.astype(jnp.float32)
    slab_ids = (jnp.arange(NAUX, dtype=jnp.int32) // PH).astype(jnp.int32)

    def aux_step(totals, inputs):
        coulomb, exchange_sum = totals
        tensor_row, slab = inputs
        block_bits = block_mask[slab]
        wide_mask = jnp.repeat(jnp.repeat(block_bits, BLK, axis=0), BLK, axis=1).astype(jnp.bfloat16)
        masked = tensor_row * wide_mask
        masked_f = masked.astype(jnp.float32)
        products = jnp.dot(masked_f, c_full, precision=lax.Precision.HIGHEST).astype(jnp.bfloat16)
        product_f = products.astype(jnp.float32)
        density = (2.0 * jnp.sum(product_f * c_full)).astype(jnp.bfloat16)
        coulomb = coulomb + masked_f * density.astype(jnp.float32)
        exchange_sum = exchange_sum + jnp.dot(product_f, product_f.T, precision=lax.Precision.HIGHEST)
        return ((coulomb, exchange_sum), None)
    zeros_fock = jnp.zeros((NBF, NBF), jnp.float32)
    (coulomb, exchange_sum), _ = lax.scan(aux_step, (zeros_fock, zeros_fock), (fitted_tensor, slab_ids))
    population = 2.0 * lax.optimization_barrier(jnp.sum(c_full * c_full, axis=1))
    qm_charge = nuclear - population
    centre_blocks = centres.reshape(3, NBLK, BLK)
    charge_blocks = qm_charge.reshape(NBLK, BLK)
    atom_blocks = jnp.transpose(mm_positions.reshape(3, NMMBLK, MD), (1, 0, 2))
    charge_rows = mm_charges.reshape(NMMBLK, MD)

    def mm_step(field_sum, inputs):
        atom_xyz, atom_charge, near_ids = inputs
        picker = (near_ids[:, None] == jnp.arange(NBLK, dtype=jnp.int32)[None, :]).astype(jnp.float32)
        kernel, near_q = near_kernel(picker, centre_blocks, charge_blocks, atom_xyz)
        potential = jnp.dot(near_q, kernel, precision=lax.Precision.HIGHEST)
        contrib = jnp.dot(kernel, atom_charge, precision=lax.Precision.HIGHEST).reshape(NB, BLK)
        field_sum = field_sum + jnp.dot(picker.T, contrib, precision=lax.Precision.HIGHEST)
        return (field_sum, potential)
    field_sum, potentials = lax.scan(mm_step, jnp.zeros((NBLK, BLK), jnp.float32), (atom_blocks, charge_rows, neighbours))
    field_vec = field_sum.reshape(NBF)
    fock = coulomb - 0.5 * exchange_sum + jnp.diag(field_vec)
    return (fock, potentials.reshape(NMM))
```

```python
import functools

import jax
import jax.numpy as jnp
from jax import lax
from jax.experimental import pallas as pl
from jax.experimental.pallas import tpu as pltpu
from jax.sharding import PartitionSpec as P

BLK = 128
VMEM_LIMIT = 48 * 1024 * 1024

softening = 1.0


def near_kernel(picker, centre_blocks, charge_blocks, atom_xyz):
    near_xyz = jnp.einsum("kb,cbj->ckj", picker, centre_blocks, precision=lax.Precision.HIGHEST)
    near_xyz = near_xyz.reshape(3, picker.shape[0] * centre_blocks.shape[2])
    near_q = jnp.dot(picker, charge_blocks, precision=lax.Precision.HIGHEST).reshape(-1)
    offsets = near_xyz[:, :, None] - atom_xyz[:, None, :]
    kernel = lax.rsqrt(jnp.sum(offsets * offsets, axis=0) + softening)
    return (kernel, near_q)


def products_kernel(t_ref, mask_ref, win_ref, c_ref, x_ref, dens_ref):
    parts, rows, cols = t_ref.shape
    row_mask = mask_ref[0]

    @pl.when(pl.program_id(0) == 0)
    def _():
        dens_ref[...] = jnp.zeros_like(dens_ref)

    own = c_ref[...].astype(jnp.float32)
    for p in range(parts):
        prod = jnp.dot(t_ref[p] * row_mask, win_ref[...], preferred_element_type=jnp.float32)
        x_ref[p] = prod.astype(x_ref.dtype)
        dens_ref[p] += jnp.sum((prod * own).reshape(rows // 8, 8, prod.shape[1]), axis=0)


def products_call(fitted, mask_rows, window_c, own_c):
    parts, rows, cols = fitted.shape
    nocc = window_c.shape[1]
    return pl.pallas_call(
        products_kernel,
        grid=(rows // BLK,),
        in_specs=[
            pl.BlockSpec((parts, BLK, cols), lambda i: (0, i, 0)),
            pl.BlockSpec((1, 1, cols), lambda i: (i, 0, 0)),
            pl.BlockSpec((cols, nocc), lambda i: (0, 0)),
            pl.BlockSpec((BLK, nocc), lambda i: (i, 0)),
        ],
        out_specs=[
            pl.BlockSpec((parts, BLK, nocc), lambda i: (0, i, 0)),
            pl.BlockSpec((parts, 8, nocc), lambda i: (0, 0, 0)),
        ],
        out_shape=[
            jax.ShapeDtypeStruct((parts, rows, nocc), jnp.bfloat16),
            jax.ShapeDtypeStruct((parts, 8, nocc), jnp.float32),
        ],
        compiler_params=pltpu.CompilerParams(vmem_limit_bytes=VMEM_LIMIT),
        cost_estimate=pl.CostEstimate(
            flops=2 * parts * rows * cols * nocc,
            bytes_accessed=2 * parts * rows * (cols + nocc),
            transcendentals=0,
        ),
        name="products",
    )(fitted, mask_rows, window_c, own_c)


def coulomb_kernel(dens_ref, t_ref, mask_ref, out_ref):
    parts = t_ref.shape[0]
    total = t_ref[0].astype(jnp.float32) * dens_ref[0]
    for p in range(1, parts):
        total += t_ref[p].astype(jnp.float32) * dens_ref[p]
    out_ref[...] = (total * mask_ref[0].astype(jnp.float32)).astype(out_ref.dtype)


def coulomb_call(densities, fitted, mask_rows):
    parts, rows, cols = fitted.shape
    return pl.pallas_call(
        coulomb_kernel,
        grid=(rows // BLK,),
        in_specs=[
            pl.BlockSpec(memory_space=pltpu.SMEM),
            pl.BlockSpec((parts, BLK, cols), lambda i: (0, i, 0)),
            pl.BlockSpec((1, 1, cols), lambda i: (i, 0, 0)),
        ],
        out_specs=pl.BlockSpec((BLK, cols), lambda i: (i, 0)),
        out_shape=jax.ShapeDtypeStruct((rows, cols), jnp.bfloat16),
        compiler_params=pltpu.CompilerParams(vmem_limit_bytes=VMEM_LIMIT),
        cost_estimate=pl.CostEstimate(
            flops=2 * parts * rows * cols,
            bytes_accessed=2 * rows * cols * (parts + 1),
            transcendentals=0,
        ),
        name="coulomb",
    )(densities, fitted, mask_rows)


def fock_kernel(place_ref, own_ref, all_ref, coul_ref, field_ref, out_ref):
    parts = own_ref.shape[0]
    rows, cols = out_ref.shape
    half = rows // 2
    dims = (((1,), (1,)), ((), ()))
    total = lax.dot_general(own_ref[0], all_ref[0], dims, preferred_element_type=jnp.float32)
    for p in range(1, parts):
        total += lax.dot_general(own_ref[p], all_ref[p], dims, preferred_element_type=jnp.float32)
    out_ref[...] = -0.5 * total
    first_row = pl.multiple_of(place_ref[0] * half, half)
    out_ref[pl.ds(first_row, half), :] += coul_ref[0].astype(jnp.float32)

    col0 = pl.program_id(0) * cols
    row0 = place_ref[1]

    @pl.when((place_ref[0] == 0) & (row0 < col0 + cols) & (row0 + rows > col0))
    def _():
        row_ids = row0 + lax.broadcasted_iota(jnp.int32, (rows, cols), 0)
        col_ids = col0 + lax.broadcasted_iota(jnp.int32, (rows, cols), 1)
        out_ref[...] += jnp.where(row_ids == col_ids, field_ref[...], jnp.float32(0.0))


def fock_call(place, x_own, x_all, coul, field_col):
    parts, rows, nocc = x_own.shape
    total = x_all.shape[1]
    per_src = coul.shape[2]
    cols = min(1024, per_src)
    step = per_src // cols
    return pl.pallas_call(
        fock_kernel,
        grid=(total // cols,),
        in_specs=[
            pl.BlockSpec(memory_space=pltpu.SMEM),
            pl.BlockSpec((parts, rows, nocc), lambda j: (0, 0, 0)),
            pl.BlockSpec((parts, cols, nocc), lambda j: (0, j, 0)),
            pl.BlockSpec((1, rows // 2, cols), lambda j: (j // step, 0, j % step)),
            pl.BlockSpec((rows, 1), lambda j: (0, 0)),
        ],
        out_specs=pl.BlockSpec((rows, cols), lambda j: (0, j)),
        out_shape=jax.ShapeDtypeStruct((rows, total), jnp.float32),
        compiler_params=pltpu.CompilerParams(vmem_limit_bytes=VMEM_LIMIT),
        cost_estimate=pl.CostEstimate(
            flops=2 * parts * rows * total * nocc,
            bytes_accessed=2 * parts * total * nocc + 4 * rows * total + rows * total,
            transcendentals=0,
        ),
        name="fock",
    )(place, x_own, x_all, coul, field_col)


def per_device(
    fitted_tensor, block_mask, orbitals, nuclear, centres, mm_positions, mm_charges, neighbours
):
    parts, row_span, col_span = fitted_tensor.shape
    nocc = orbitals.shape[1]
    orb_count = lax.axis_size("orb")
    aux_count = lax.axis_size("aux")
    grp_id = lax.axis_index("grp")
    aux_id = lax.axis_index("aux")
    orb_id = lax.axis_index("orb")
    own_span = row_span // orb_count
    half = own_span // 2
    block_total = block_mask.shape[1]
    row_start = aux_id * row_span
    col_start = orb_id * col_span

    if aux_count == orb_count:
        perm = [
            (a * orb_count + o, o * orb_count + a)
            for a in range(aux_count)
            for o in range(orb_count)
        ]
        window_c = lax.ppermute(orbitals, ("aux", "orb"), perm)
    else:
        whole_c = lax.all_gather(orbitals, "aux", axis=0, tiled=True)
        window_c = lax.dynamic_slice_in_dim(whole_c, col_start, col_span, 0)

    bits = lax.dynamic_slice(
        block_mask[0],
        (row_start // BLK, col_start // BLK),
        (row_span // BLK, col_span // BLK),
    ).astype(jnp.bfloat16)
    mask_rows = jnp.repeat(bits, BLK, axis=1)[:, None, :]

    x_part, dens_lanes = products_call(fitted_tensor, mask_rows, window_c, orbitals)
    dens_part = 2.0 * jnp.sum(dens_lanes, axis=(1, 2))
    densities = lax.psum(dens_part, ("aux", "orb")).astype(jnp.bfloat16).astype(jnp.float32)

    x_swap = lax.all_to_all(
        x_part.reshape(parts, orb_count, own_span, nocc), "orb", split_axis=1, concat_axis=1, tiled=True
    )
    x_own = jnp.sum(x_swap.astype(jnp.float32), axis=1).astype(jnp.bfloat16)
    x_all = lax.all_gather(x_own, ("aux", "orb"), axis=1, tiled=True)

    coul = coulomb_call(densities, fitted_tensor, mask_rows)
    coul = coul.reshape(orb_count, 2, half, col_span)
    away = lax.dynamic_index_in_dim(coul, 1 - grp_id, 1, keepdims=False)
    kept = lax.dynamic_index_in_dim(coul, grp_id, 1, keepdims=False)
    got = lax.ppermute(away, "grp", [(0, 1), (1, 0)])
    both = (kept.astype(jnp.float32) + got.astype(jnp.float32)).astype(jnp.bfloat16)
    coul_rows = lax.all_to_all(both, "orb", split_axis=0, concat_axis=0, tiled=True)

    own_float = orbitals.astype(jnp.float32)
    own_population = 2.0 * jnp.sum(own_float * own_float, axis=1)
    population = lax.all_gather(own_population, "aux", axis=0, tiled=True)
    qm_charge = nuclear - population
    centre_blocks = centres.reshape(3, block_total, BLK)
    charge_blocks = qm_charge.reshape(block_total, BLK)
    picker = (neighbours[0][:, None] == jnp.arange(block_total, dtype=jnp.int32)[None, :]).astype(
        jnp.float32
    )
    kernel, near_q = near_kernel(picker, centre_blocks, charge_blocks, mm_positions)
    mm_potential = jnp.dot(near_q, kernel, precision=lax.Precision.HIGHEST)
    contrib = jnp.dot(kernel, mm_charges, precision=lax.Precision.HIGHEST).reshape(
        picker.shape[0], BLK
    )
    field_part = jnp.dot(picker.T, contrib, precision=lax.Precision.HIGHEST)
    field_vec = lax.psum(field_part, ("grp", "aux", "orb")).reshape(-1)

    own_first = row_start + orb_id * own_span
    field_col = lax.dynamic_slice_in_dim(field_vec, own_first, own_span, 0)[:, None]
    place = jnp.stack([grp_id, own_first]).astype(jnp.int32)
    fock_part = fock_call(place, x_own, x_all, coul_rows, field_col)
    fock = lax.psum(fock_part, "grp")
    return (fock, mm_potential)


def solution(mesh):
    in_specs = (
        P("grp", "aux", "orb"),
        P("grp", None, None),
        P("aux", None),
        P(),
        P(),
        P(None, ("grp", "aux", "orb")),
        P(("grp", "aux", "orb")),
        P(("grp", "aux", "orb"), None),
    )
    out_specs = (P(("aux", "orb"), None), P(("grp", "aux", "orb")))
    return jax.shard_map(
        per_device, mesh=mesh, in_specs=in_specs, out_specs=out_specs, check_vma=False
    )
```

```python
import functools

import jax
import jax.numpy as jnp
from jax import lax
from jax.experimental import pallas as pl
from jax.experimental.pallas import tpu as pltpu
from jax.sharding import PartitionSpec as P

BLK = 128
VMEM_LIMIT = 48 * 1024 * 1024

softening = 1.0


def near_kernel(picker, centre_blocks, charge_blocks, atom_xyz):
    near_xyz = jnp.einsum("kb,cbj->ckj", picker, centre_blocks, precision=lax.Precision.HIGHEST)
    near_xyz = near_xyz.reshape(3, picker.shape[0] * centre_blocks.shape[2])
    near_q = jnp.dot(picker, charge_blocks, precision=lax.Precision.HIGHEST).reshape(-1)
    offsets = near_xyz[:, :, None] - atom_xyz[:, None, :]
    kernel = lax.rsqrt(jnp.sum(offsets * offsets, axis=0) + softening)
    return (kernel, near_q)


def products_kernel(t_ref, mask_ref, win_ref, c_ref, x_ref, dens_ref):
    parts, rows, cols = t_ref.shape
    row_mask = mask_ref[0]

    @pl.when(pl.program_id(0) == 0)
    def _():
        dens_ref[...] = jnp.zeros_like(dens_ref)

    own = c_ref[...].astype(jnp.float32)
    for p in range(parts):
        prod = jnp.dot(t_ref[p] * row_mask, win_ref[...], preferred_element_type=jnp.float32)
        x_ref[p] = prod.astype(x_ref.dtype)
        dens_ref[p] += jnp.sum((prod * own).reshape(rows // 8, 8, prod.shape[1]), axis=0)


def products_call(fitted, mask_rows, window_c, own_c):
    parts, rows, cols = fitted.shape
    nocc = window_c.shape[1]
    return pl.pallas_call(
        products_kernel,
        grid=(rows // BLK,),
        in_specs=[
            pl.BlockSpec((parts, BLK, cols), lambda i: (0, i, 0)),
            pl.BlockSpec((1, 1, cols), lambda i: (i, 0, 0)),
            pl.BlockSpec((cols, nocc), lambda i: (0, 0)),
            pl.BlockSpec((BLK, nocc), lambda i: (i, 0)),
        ],
        out_specs=[
            pl.BlockSpec((parts, BLK, nocc), lambda i: (0, i, 0)),
            pl.BlockSpec((parts, 8, nocc), lambda i: (0, 0, 0)),
        ],
        out_shape=[
            jax.ShapeDtypeStruct((parts, rows, nocc), jnp.bfloat16),
            jax.ShapeDtypeStruct((parts, 8, nocc), jnp.float32),
        ],
        compiler_params=pltpu.CompilerParams(vmem_limit_bytes=VMEM_LIMIT),
        cost_estimate=pl.CostEstimate(
            flops=2 * parts * rows * cols * nocc,
            bytes_accessed=2 * parts * rows * (cols + nocc),
            transcendentals=0,
        ),
        name="products",
    )(fitted, mask_rows, window_c, own_c)


def coulomb_kernel(place_ref, dens_ref, ta_ref, ma_ref, tk_ref, mk_ref, away_ref, kept_ref):
    for t_ref, mask_ref, out_ref in ((ta_ref, ma_ref, away_ref), (tk_ref, mk_ref, kept_ref)):
        total = t_ref[0].astype(jnp.float32) * dens_ref[0]
        for p in range(1, t_ref.shape[0]):
            total += t_ref[p].astype(jnp.float32) * dens_ref[p]
        out_ref[...] = (total * mask_ref[0].astype(jnp.float32)).astype(out_ref.dtype)


def coulomb_call(place, densities, fitted, mask_rows, half):
    parts, rows, cols = fitted.shape
    tile = min(BLK, half)
    steps = half // tile

    def away_tile(i, place_ref):
        return (place_ref[1] * 2 + 1 - place_ref[0]) * steps + i

    def kept_tile(i, place_ref):
        return (place_ref[1] * 2 + place_ref[0]) * steps + i

    def tensor_spec(which):
        return pl.BlockSpec((parts, tile, cols), lambda i, place_ref, d: (0, which(i, place_ref), 0))

    def mask_spec(which):
        return pl.BlockSpec(
            (1, 1, cols), lambda i, place_ref, d: (which(i, place_ref) * tile // BLK, 0, 0)
        )

    return pl.pallas_call(
        coulomb_kernel,
        grid_spec=pltpu.PrefetchScalarGridSpec(
            num_scalar_prefetch=2,
            grid=(steps,),
            in_specs=[
                tensor_spec(away_tile),
                mask_spec(away_tile),
                tensor_spec(kept_tile),
                mask_spec(kept_tile),
            ],
            out_specs=[pl.BlockSpec((tile, cols), lambda i, place_ref, d: (i, 0))] * 2,
        ),
        out_shape=[jax.ShapeDtypeStruct((half, cols), jnp.bfloat16)] * 2,
        compiler_params=pltpu.CompilerParams(vmem_limit_bytes=VMEM_LIMIT),
        cost_estimate=pl.CostEstimate(
            flops=4 * parts * half * cols,
            bytes_accessed=4 * half * cols * (parts + 1),
            transcendentals=0,
        ),
        name="coulomb",
    )(place, densities, fitted, mask_rows, fitted, mask_rows)


def fock_kernel(shifts, place_ref, own_ref, mate_ref, all_ref, mate_all_ref, field_ref, *refs):
    mine, theirs, out_ref = refs[:shifts], refs[shifts : 2 * shifts], refs[2 * shifts]
    parts = own_ref.shape[0]
    rows, cols = out_ref.shape
    half = rows // 2
    per_src = mine[0].shape[1] // cols
    dims = (((1,), (1,)), ((), ()))
    grp_id, row0, orb_id = place_ref[0], place_ref[1], place_ref[2]

    def slab(a, b):
        total = lax.dot_general(a[0], b[0], dims, preferred_element_type=jnp.float32)
        for p in range(1, parts):
            total += lax.dot_general(a[p], b[p], dims, preferred_element_type=jnp.float32)
        return total

    out_ref[...] = -0.5 * (slab(own_ref, all_ref) + slab(mate_ref, mate_all_ref))

    step = pl.program_id(0)
    shift = lax.rem(orb_id - step // per_src + shifts, shifts)
    col_in = pl.multiple_of(lax.rem(step, per_src) * cols, cols)
    own_row = pl.multiple_of(grp_id * half, half)
    mate_row = pl.multiple_of((1 - grp_id) * half, half)
    for k in range(shifts):

        @pl.when(shift == k)
        def _():
            out_ref[pl.ds(own_row, half), :] += mine[k][:, pl.ds(col_in, cols)].astype(jnp.float32)
            out_ref[pl.ds(mate_row, half), :] += theirs[k][:, pl.ds(col_in, cols)].astype(jnp.float32)

    col0 = step * cols

    @pl.when((row0 < col0 + cols) & (row0 + rows > col0))
    def _():
        row_ids = row0 + lax.broadcasted_iota(jnp.int32, (rows, cols), 0)
        col_ids = col0 + lax.broadcasted_iota(jnp.int32, (rows, cols), 1)
        out_ref[...] += jnp.where(row_ids == col_ids, field_ref[...], jnp.float32(0.0))


def fock_call(place, x_own, x_mate, x_all, x_mate_all, field_col, mine, theirs):
    parts, rows, nocc = x_own.shape
    total = x_all.shape[1]
    half, per_src = mine[0].shape
    cols = min(1024, per_src)
    own_spec = pl.BlockSpec((parts, rows, nocc), lambda j: (0, 0, 0))
    all_spec = pl.BlockSpec((parts, cols, nocc), lambda j: (0, j, 0))
    return pl.pallas_call(
        functools.partial(fock_kernel, len(mine)),
        grid=(total // cols,),
        in_specs=[
            pl.BlockSpec(memory_space=pltpu.SMEM),
            own_spec,
            own_spec,
            all_spec,
            all_spec,
            pl.BlockSpec((rows, 1), lambda j: (0, 0)),
        ]
        + [pl.BlockSpec((half, per_src), lambda j: (0, 0))] * (2 * len(mine)),
        out_specs=pl.BlockSpec((rows, cols), lambda j: (0, j)),
        out_shape=jax.ShapeDtypeStruct((rows, total), jnp.float32),
        compiler_params=pltpu.CompilerParams(vmem_limit_bytes=VMEM_LIMIT),
        cost_estimate=pl.CostEstimate(
            flops=4 * parts * rows * total * nocc,
            bytes_accessed=4 * parts * total * nocc + 4 * rows * total + 2 * rows * total,
            transcendentals=0,
        ),
        name="fock",
    )(place, x_own, x_mate, x_all, x_mate_all, field_col, *mine, *theirs)


def swap(value):
    return lax.ppermute(value, "grp", [(0, 1), (1, 0)])


def per_device(
    fitted_tensor, block_mask, orbitals, nuclear, centres, mm_positions, mm_charges, neighbours
):
    parts, row_span, col_span = fitted_tensor.shape
    nocc = orbitals.shape[1]
    orb_count = lax.axis_size("orb")
    aux_count = lax.axis_size("aux")
    grp_count = lax.axis_size("grp")
    grp_id = lax.axis_index("grp")
    aux_id = lax.axis_index("aux")
    orb_id = lax.axis_index("orb")
    own_span = row_span // orb_count
    half = own_span // 2
    block_total = block_mask.shape[1]
    row_start = aux_id * row_span
    col_start = orb_id * col_span

    if aux_count == orb_count:
        perm = [
            (a * orb_count + o, o * orb_count + a)
            for a in range(aux_count)
            for o in range(orb_count)
        ]
        c_half = lax.dynamic_slice_in_dim(orbitals, grp_id * (row_span // 2), row_span // 2, 0)
        c_half = lax.ppermute(c_half, ("aux", "orb"), perm)
        c_mate = swap(c_half)
        window_c = jnp.where(
            grp_id == 0, jnp.stack([c_half, c_mate]), jnp.stack([c_mate, c_half])
        ).reshape(col_span, nocc)
    else:
        whole_c = lax.all_gather(orbitals, "aux", axis=0, tiled=True)
        window_c = lax.dynamic_slice_in_dim(whole_c, col_start, col_span, 0)

    bits = lax.dynamic_slice(
        block_mask[0],
        (row_start // BLK, col_start // BLK),
        (row_span // BLK, col_span // BLK),
    ).astype(jnp.bfloat16)
    mask_rows = jnp.repeat(bits, BLK, axis=1)[:, None, :]

    own_float = orbitals.astype(jnp.float32)
    own_population = 2.0 * jnp.sum(own_float * own_float, axis=1)
    population = lax.all_gather(own_population, "aux", axis=0, tiled=True)
    qm_charge = nuclear - population
    centre_blocks = centres.reshape(3, block_total, BLK)
    charge_blocks = qm_charge.reshape(block_total, BLK)
    picker = (neighbours[0][:, None] == jnp.arange(block_total, dtype=jnp.int32)[None, :]).astype(
        jnp.float32
    )
    kernel, near_q = near_kernel(picker, centre_blocks, charge_blocks, mm_positions)
    mm_potential = jnp.dot(near_q, kernel, precision=lax.Precision.HIGHEST)
    contrib = jnp.dot(kernel, mm_charges, precision=lax.Precision.HIGHEST).reshape(
        picker.shape[0], BLK
    )
    field_part = jnp.dot(picker.T, contrib, precision=lax.Precision.HIGHEST)

    x_part, dens_lanes = products_call(fitted_tensor, mask_rows, window_c, orbitals)
    dens_part = 2.0 * jnp.sum(dens_lanes, axis=(1, 2))
    dens_slots = jnp.zeros((grp_count, BLK), jnp.float32)
    dens_slots = lax.dynamic_update_slice(dens_slots, dens_part[None, :], (grp_id, 0))
    sums = lax.psum(jnp.concatenate([field_part, dens_slots], axis=0), ("grp", "aux", "orb"))
    field_vec = sums[:block_total].reshape(-1)
    densities = lax.dynamic_slice(sums, (block_total + grp_id, 0), (1, parts))[0]

    x_blocks = x_part.reshape(parts, orb_count, own_span, nocc)
    x_sum = lax.dynamic_index_in_dim(x_blocks, orb_id, 1, keepdims=False).astype(jnp.float32)
    mine, theirs = [], []
    targets = [lax.rem(orb_id + k, orb_count) for k in range(orb_count)]
    moves = [[(s, (s + k) % orb_count) for s in range(orb_count)] for k in range(orb_count)]
    for k in range(1, orb_count):
        block = lax.dynamic_index_in_dim(x_blocks, targets[k], 1, keepdims=False)
        x_sum += lax.ppermute(block, "orb", moves[k]).astype(jnp.float32)
    x_own = x_sum.astype(jnp.bfloat16)
    x_mate = swap(x_own)
    x_all = lax.all_gather(x_own, ("aux", "orb"), axis=1, tiled=True)
    x_mate_all = swap(x_all)

    mine, theirs = [None] * orb_count, [None] * orb_count
    for k in list(range(1, orb_count)) + [0]:
        at = jnp.stack([grp_id, targets[k]]).astype(jnp.int32)
        away, kept = coulomb_call(at, densities, fitted_tensor, mask_rows, half)
        both = (kept.astype(jnp.float32) + swap(away).astype(jnp.float32)).astype(jnp.bfloat16)
        mine[k] = lax.ppermute(both, "orb", moves[k]) if k else both
        theirs[k] = swap(mine[k])

    own_first = row_start + orb_id * own_span
    field_col = lax.dynamic_slice_in_dim(field_vec, own_first, own_span, 0)[:, None]
    place = jnp.stack([grp_id, own_first, orb_id]).astype(jnp.int32)
    fock = fock_call(place, x_own, x_mate, x_all, x_mate_all, field_col, mine, theirs)
    return (fock, mm_potential)


def solution(mesh):
    in_specs = (
        P("grp", "aux", "orb"),
        P("grp", None, None),
        P("aux", None),
        P(),
        P(),
        P(None, ("grp", "aux", "orb")),
        P(("grp", "aux", "orb")),
        P(("grp", "aux", "orb"), None),
    )
    out_specs = (P(("aux", "orb"), None), P(("grp", "aux", "orb")))
    return jax.shard_map(
        per_device, mesh=mesh, in_specs=in_specs, out_specs=out_specs, check_vma=False
    )
```

```python
import functools

import jax
import jax.numpy as jnp
from jax import lax
from jax.experimental import pallas as pl
from jax.experimental.pallas import tpu as pltpu
from jax.sharding import PartitionSpec as P

BLK = 128
VMEM_LIMIT = 48 * 1024 * 1024

softening = 1.0


def near_kernel(picker, centre_blocks, atom_xyz):
    near_xyz = jnp.einsum("kb,cbj->ckj", picker, centre_blocks, precision=lax.Precision.HIGHEST)
    near_xyz = near_xyz.reshape(3, picker.shape[0] * centre_blocks.shape[2])
    offsets = near_xyz[:, :, None] - atom_xyz[:, None, :]
    return lax.rsqrt(jnp.sum(offsets * offsets, axis=0) + softening)


def products_kernel(t_ref, mask_ref, win_ref, c_ref, x_ref, dens_ref):
    parts, rows, cols = t_ref.shape
    row_mask = mask_ref[0]

    @pl.when(pl.program_id(0) == 0)
    def _():
        dens_ref[...] = jnp.zeros_like(dens_ref)

    own = c_ref[...].astype(jnp.float32)
    for p in range(parts):
        prod = jnp.dot(t_ref[p] * row_mask, win_ref[...], preferred_element_type=jnp.float32)
        x_ref[p] = prod.astype(x_ref.dtype)
        dens_ref[p] += jnp.sum((prod * own).reshape(rows // 8, 8, prod.shape[1]), axis=0)


def products_call(fitted, mask_rows, window_c, own_c):
    parts, rows, cols = fitted.shape
    nocc = window_c.shape[1]
    return pl.pallas_call(
        products_kernel,
        grid=(rows // BLK,),
        in_specs=[
            pl.BlockSpec((parts, BLK, cols), lambda i: (0, i, 0)),
            pl.BlockSpec((1, 1, cols), lambda i: (i, 0, 0)),
            pl.BlockSpec((cols, nocc), lambda i: (0, 0)),
            pl.BlockSpec((BLK, nocc), lambda i: (i, 0)),
        ],
        out_specs=[
            pl.BlockSpec((parts, BLK, nocc), lambda i: (0, i, 0)),
            pl.BlockSpec((parts, 8, nocc), lambda i: (0, 0, 0)),
        ],
        out_shape=[
            jax.ShapeDtypeStruct((parts, rows, nocc), jnp.bfloat16),
            jax.ShapeDtypeStruct((parts, 8, nocc), jnp.float32),
        ],
        compiler_params=pltpu.CompilerParams(vmem_limit_bytes=VMEM_LIMIT),
        cost_estimate=pl.CostEstimate(
            flops=2 * parts * rows * cols * nocc,
            bytes_accessed=2 * parts * rows * (cols + nocc),
            transcendentals=0,
        ),
        name="products",
    )(fitted, mask_rows, window_c, own_c)


def coulomb_kernel(place_ref, dens_ref, ta_ref, ma_ref, tk_ref, mk_ref, away_ref, kept_ref):
    for t_ref, mask_ref, out_ref in ((ta_ref, ma_ref, away_ref), (tk_ref, mk_ref, kept_ref)):
        total = t_ref[0].astype(jnp.float32) * dens_ref[0]
        for p in range(1, t_ref.shape[0]):
            total += t_ref[p].astype(jnp.float32) * dens_ref[p]
        out_ref[...] = (total * mask_ref[0].astype(jnp.float32)).astype(out_ref.dtype)


def coulomb_call(place, densities, fitted, mask_rows, half):
    parts, rows, cols = fitted.shape
    tile = min(BLK, half)
    steps = half // tile

    def away_tile(i, place_ref):
        return (place_ref[1] * 2 + 1 - place_ref[0]) * steps + i

    def kept_tile(i, place_ref):
        return (place_ref[1] * 2 + place_ref[0]) * steps + i

    def tensor_spec(which):
        return pl.BlockSpec((parts, tile, cols), lambda i, place_ref, d: (0, which(i, place_ref), 0))

    def mask_spec(which):
        return pl.BlockSpec(
            (1, 1, cols), lambda i, place_ref, d: (which(i, place_ref) * tile // BLK, 0, 0)
        )

    return pl.pallas_call(
        coulomb_kernel,
        grid_spec=pltpu.PrefetchScalarGridSpec(
            num_scalar_prefetch=2,
            grid=(steps,),
            in_specs=[
                tensor_spec(away_tile),
                mask_spec(away_tile),
                tensor_spec(kept_tile),
                mask_spec(kept_tile),
            ],
            out_specs=[pl.BlockSpec((tile, cols), lambda i, place_ref, d: (i, 0))] * 2,
        ),
        out_shape=[jax.ShapeDtypeStruct((half, cols), jnp.bfloat16)] * 2,
        compiler_params=pltpu.CompilerParams(vmem_limit_bytes=VMEM_LIMIT),
        cost_estimate=pl.CostEstimate(
            flops=4 * parts * half * cols,
            bytes_accessed=4 * half * cols * (parts + 1),
            transcendentals=0,
        ),
        name="coulomb",
    )(place, densities, fitted, mask_rows, fitted, mask_rows)


def fock_kernel(shifts, place_ref, own_ref, mate_ref, all_ref, mate_all_ref, field_ref, *refs):
    mine, theirs, out_ref = refs[:shifts], refs[shifts : 2 * shifts], refs[2 * shifts]
    parts = own_ref.shape[0]
    rows, cols = out_ref.shape
    half = rows // 2
    per_src = mine[0].shape[1] // cols
    dims = (((1,), (1,)), ((), ()))
    grp_id, row0, orb_id = place_ref[0], place_ref[1], place_ref[2]

    def slab(a, b):
        total = lax.dot_general(a[0], b[0], dims, preferred_element_type=jnp.float32)
        for p in range(1, parts):
            total += lax.dot_general(a[p], b[p], dims, preferred_element_type=jnp.float32)
        return total

    out_ref[...] = -0.5 * (slab(own_ref, all_ref) + slab(mate_ref, mate_all_ref))

    step = pl.program_id(0)
    shift = lax.rem(orb_id - step // per_src + shifts, shifts)
    col_in = pl.multiple_of(lax.rem(step, per_src) * cols, cols)
    own_row = pl.multiple_of(grp_id * half, half)
    mate_row = pl.multiple_of((1 - grp_id) * half, half)
    for k in range(shifts):

        @pl.when(shift == k)
        def _():
            out_ref[pl.ds(own_row, half), :] += mine[k][:, pl.ds(col_in, cols)].astype(jnp.float32)
            out_ref[pl.ds(mate_row, half), :] += theirs[k][:, pl.ds(col_in, cols)].astype(jnp.float32)

    col0 = step * cols

    @pl.when((row0 < col0 + cols) & (row0 + rows > col0))
    def _():
        row_ids = row0 + lax.broadcasted_iota(jnp.int32, (rows, cols), 0)
        col_ids = col0 + lax.broadcasted_iota(jnp.int32, (rows, cols), 1)
        out_ref[...] += jnp.where(row_ids == col_ids, field_ref[...], jnp.float32(0.0))


def fock_call(place, x_own, x_mate, x_all, x_mate_all, field_col, mine, theirs):
    parts, rows, nocc = x_own.shape
    total = x_all.shape[1]
    half, per_src = mine[0].shape
    cols = min(1024, per_src)
    own_spec = pl.BlockSpec((parts, rows, nocc), lambda j: (0, 0, 0))
    all_spec = pl.BlockSpec((parts, cols, nocc), lambda j: (0, j, 0))
    return pl.pallas_call(
        functools.partial(fock_kernel, len(mine)),
        grid=(total // cols,),
        in_specs=[
            pl.BlockSpec(memory_space=pltpu.SMEM),
            own_spec,
            own_spec,
            all_spec,
            all_spec,
            pl.BlockSpec((rows, 1), lambda j: (0, 0)),
        ]
        + [pl.BlockSpec((half, per_src), lambda j: (0, 0))] * (2 * len(mine)),
        out_specs=pl.BlockSpec((rows, cols), lambda j: (0, j)),
        out_shape=jax.ShapeDtypeStruct((rows, total), jnp.float32),
        compiler_params=pltpu.CompilerParams(vmem_limit_bytes=VMEM_LIMIT),
        cost_estimate=pl.CostEstimate(
            flops=4 * parts * rows * total * nocc,
            bytes_accessed=4 * parts * total * nocc + 4 * rows * total + 2 * rows * total,
            transcendentals=0,
        ),
        name="fock",
    )(place, x_own, x_mate, x_all, x_mate_all, field_col, *mine, *theirs)


def swap(value):
    return lax.ppermute(value, "grp", [(0, 1), (1, 0)])


def per_device(
    fitted_tensor, block_mask, orbitals, nuclear, centres, mm_positions, mm_charges, neighbours
):
    parts, row_span, col_span = fitted_tensor.shape
    nocc = orbitals.shape[1]
    orb_count = lax.axis_size("orb")
    aux_count = lax.axis_size("aux")
    grp_count = lax.axis_size("grp")
    grp_id = lax.axis_index("grp")
    aux_id = lax.axis_index("aux")
    orb_id = lax.axis_index("orb")
    own_span = row_span // orb_count
    half = own_span // 2
    block_total = block_mask.shape[1]
    row_start = aux_id * row_span
    col_start = orb_id * col_span

    if aux_count == orb_count:
        perm = [
            (a * orb_count + o, o * orb_count + a)
            for a in range(aux_count)
            for o in range(orb_count)
        ]
        c_half = lax.dynamic_slice_in_dim(orbitals, grp_id * (row_span // 2), row_span // 2, 0)
        c_half = lax.ppermute(c_half, ("aux", "orb"), perm)
        c_mate = swap(c_half)
        window_c = jnp.where(
            grp_id == 0, jnp.stack([c_half, c_mate]), jnp.stack([c_mate, c_half])
        ).reshape(col_span, nocc)
    else:
        whole_c = lax.all_gather(orbitals, "aux", axis=0, tiled=True)
        window_c = lax.dynamic_slice_in_dim(whole_c, col_start, col_span, 0)

    bits = lax.dynamic_slice(
        block_mask[0],
        (row_start // BLK, col_start // BLK),
        (row_span // BLK, col_span // BLK),
    ).astype(jnp.bfloat16)
    mask_rows = jnp.repeat(bits, BLK, axis=1)[:, None, :]

    own_float = orbitals.astype(jnp.float32)
    own_population = 2.0 * jnp.sum(own_float * own_float, axis=1)
    population = lax.all_gather(own_population, "aux", axis=0, tiled=True)
    centre_blocks = centres.reshape(3, block_total, BLK)
    picker = (neighbours[0][:, None] == jnp.arange(block_total, dtype=jnp.int32)[None, :]).astype(
        jnp.float32
    )
    kernel = near_kernel(picker, centre_blocks, mm_positions)
    contrib = jnp.dot(kernel, mm_charges, precision=lax.Precision.HIGHEST).reshape(
        picker.shape[0], BLK
    )
    field_part = jnp.dot(picker.T, contrib, precision=lax.Precision.HIGHEST)

    window_c, population = lax.optimization_barrier((window_c, population))
    qm_charge = nuclear - population
    charge_blocks = qm_charge.reshape(block_total, BLK)
    near_q = jnp.dot(picker, charge_blocks, precision=lax.Precision.HIGHEST).reshape(-1)
    mm_potential = jnp.dot(near_q, kernel, precision=lax.Precision.HIGHEST)

    x_part, dens_lanes = products_call(fitted_tensor, mask_rows, window_c, orbitals)
    dens_part = 2.0 * jnp.sum(dens_lanes, axis=(1, 2))
    dens_slots = jnp.zeros((grp_count, BLK), jnp.float32)
    dens_slots = lax.dynamic_update_slice(dens_slots, dens_part[None, :], (grp_id, 0))
    sums = lax.psum(jnp.concatenate([field_part, dens_slots], axis=0), ("grp", "aux", "orb"))

    x_blocks = x_part.reshape(parts, orb_count, own_span, nocc)
    targets = [lax.rem(orb_id + k, orb_count) for k in range(orb_count)]
    moves = [[(s, (s + k) % orb_count) for s in range(orb_count)] for k in range(orb_count)]
    arrived = []
    for k in range(1, orb_count):
        block = lax.dynamic_index_in_dim(x_blocks, targets[k], 1, keepdims=False)
        arrived.append(lax.ppermute(block, "orb", moves[k]))
    sums, *arrived = lax.optimization_barrier((sums, *arrived))
    field_vec = sums[:block_total].reshape(-1)
    densities = lax.dynamic_slice(sums, (block_total + grp_id, 0), (1, parts))[0]
    x_sum = lax.dynamic_index_in_dim(x_blocks, orb_id, 1, keepdims=False).astype(jnp.float32)
    for block in arrived:
        x_sum += block.astype(jnp.float32)
    x_own = x_sum.astype(jnp.bfloat16)
    x_mate = swap(x_own)
    x_all = lax.all_gather(x_own, ("aux", "orb"), axis=1, tiled=True)

    mine = [None] * orb_count
    for k in list(range(1, orb_count)) + [0]:
        at = jnp.stack([grp_id, targets[k]]).astype(jnp.int32)
        away, kept = coulomb_call(at, densities, fitted_tensor, mask_rows, half)
        both = (kept.astype(jnp.float32) + swap(away).astype(jnp.float32)).astype(jnp.bfloat16)
        mine[k] = lax.ppermute(both, "orb", moves[k]) if k else both
    x_all, *mine = lax.optimization_barrier((x_all, *mine))
    theirs = [swap(block) for block in mine]
    x_mate_all = swap(x_all)

    own_first = row_start + orb_id * own_span
    field_col = lax.dynamic_slice_in_dim(field_vec, own_first, own_span, 0)[:, None]
    place = jnp.stack([grp_id, own_first, orb_id]).astype(jnp.int32)
    fock = fock_call(place, x_own, x_mate, x_all, x_mate_all, field_col, mine, theirs)
    return (fock, mm_potential)


def solution(mesh):
    in_specs = (
        P("grp", "aux", "orb"),
        P("grp", None, None),
        P("aux", None),
        P(),
        P(),
        P(None, ("grp", "aux", "orb")),
        P(("grp", "aux", "orb")),
        P(("grp", "aux", "orb"), None),
    )
    out_specs = (P(("aux", "orb"), None), P(("grp", "aux", "orb")))
    return jax.shard_map(
        per_device, mesh=mesh, in_specs=in_specs, out_specs=out_specs, check_vma=False
    )
```
